32 devices in a mesh: slab: 4 (over z), region: 8 (over y, x, core).
Axes of the slice: x: 2, y: 2, z: 4, core: 2. Of those that a mesh axis runs over, the one named last changes fastest.
Arguments:
- prior_matrix: float32 [256, 65536], P('region', 'slab'), may hold values from -6 to 6
- prior_at_measurements: float32 [256, 8192], P('region', 'slab'), may hold values from -6 to 6
- scaled_residual_vector: float32 [256, 8192], P('region', 'slab'), may hold values from -6 to 6
- lattice_coordinates: float32 [2, 65536], P(None, 'slab'), may hold values from 0 to 2
- measurement_coordinates: float32 [2, 8192], replicated, may hold values from 0 to 2
- neighbour_block_totals: int32 [512], P('slab'), may hold values from 2 to 16, as said below
- neighbour_block_numbers: int32 [512, 16], P('slab'), may hold values from 0 to 19, as said below
Outputs:
- analysis: float32 [256, 65536], P('region', 'slab')
The draws below stay inside these ranges and needn't reach their ends.
Inputs may be any that keep to these rules, and one draw needn't show every extreme that they name: neighbour_block_totals[t] observation tiles are listed for grid tile t; in every slab some grid tile lists 16 and some lists 2. `neighbour_block_numbers`: row t's first neighbour_block_totals[t] entries are distinct, and each names an observation tile s * 16 - 2 + e that exists (from 0 to 16 * 4 - 1), s being t's slab; the remaining entries of the row are 0.
All inputs are finite; a program needn't handle non-finite values.
Results may differ from the reference program's by a relative error of at most 0.0003.
Values sent between devices are 32-bit elements; how exact they have to be, the bound alone decides.
A program may use at most 64 MiB of HBM per device.

```python
import jax
import jax.numpy as jnp
from jax import lax

MEMBERSHIP_TOTAL = 256
BLOCK_NODES = 128
OBS_TILE = 128
TILES_REGION = 16
OBS_SLAB = 16
EDGE = 2
LIST_MOST = 16
TILES_SLAB = 128
GRID_TILES = 512
LATTICE_NODES = 65536
MEASUREMENTS = 8192


def block_order(subkey):
    return jax.random.permutation(subkey, TILES_SLAB // TILES_REGION)


def counts_helper(key):
    base_key = jax.random.fold_in(key, 7)
    slabs = GRID_TILES // TILES_SLAB
    regions = TILES_SLAB // TILES_REGION
    dense_count = max(1, regions // 4)
    subkeys = jax.random.split(base_key, 3)
    block_rank = jax.vmap(block_order)(jax.random.split(subkeys[0], slabs))
    dense = block_rank < dense_count
    dense_tiles = jnp.repeat(dense, TILES_REGION, axis=1)
    high_draw = jax.random.randint(subkeys[1], (slabs, TILES_SLAB), LIST_MOST * 3 // 4, LIST_MOST + 1)
    low_draw = jax.random.randint(subkeys[2], (slabs, TILES_SLAB), 2, max(3, LIST_MOST // 2))
    counts = jnp.where(dense_tiles, high_draw, low_draw)
    counts = counts.at[:, 0].set(LIST_MOST)
    counts = counts.at[:, 1].set(2)
    return counts.reshape(GRID_TILES).astype(jnp.int32)


def draw_neighbour_block_totals(key, part):
    return counts_helper(key)


def draw_neighbour_block_numbers(key, part):
    counts = counts_helper(key)
    extended = OBS_SLAB + 2 * EDGE
    slabs = GRID_TILES // TILES_SLAB
    tile_slab = jnp.arange(GRID_TILES, dtype=jnp.int32) // TILES_SLAB
    ext_ids = jnp.arange(extended, dtype=jnp.int32)[None, :]
    global_tile = tile_slab[:, None] * OBS_SLAB - EDGE + ext_ids
    valid = (global_tile >= 0) & (global_tile < OBS_SLAB * slabs)
    scores = jax.random.randint(jax.random.fold_in(key, 11), (GRID_TILES, extended), 0, 1 << 16) * extended + ext_ids
    scores = jnp.where(valid, scores, scores + (1 << 26))
    picked = jnp.argsort(scores, axis=1)[:, :LIST_MOST].astype(jnp.int32)
    used = jnp.arange(LIST_MOST, dtype=jnp.int32)[None, :] < counts[:, None]
    return jnp.where(used, picked, 0).astype(jnp.int32)


def levels(rng, extent, cuts, smallest, largest):
    loudness, own = 1.0, jax.random.fold_in(rng, 6)
    for dim, blocks in cuts:
        heights = jnp.exp(jax.random.uniform(jax.random.fold_in(own, dim), (blocks,), jnp.float32, smallest / len(cuts), largest / len(cuts)))
        loudness = loudness * jnp.repeat(heights, extent[dim] // blocks).reshape([-1 if axis == dim else 1 for axis in range(len(extent))])
    return loudness


def normal_values(stream_key, dims, scale, bound, cuts=(), held_as=jnp.bfloat16):
    values = jax.random.normal(stream_key, dims, jnp.float32) * scale
    if len(cuts) > 0:
        values = levels(stream_key, dims, cuts, -0.22, 0.18) * values
    return jnp.clip(values, min=-bound, max=bound).astype(held_as)


def setup_inputs(seed: int = 0) -> dict:
    keys = jax.random.split(jax.random.key(seed), 8)
    prior_matrix = normal_values(keys[0], (MEMBERSHIP_TOTAL, LATTICE_NODES), 1.0, 6.0, ((0, 8), (1, 4)), jnp.float32)
    prior_at_measurements = normal_values(keys[1], (MEMBERSHIP_TOTAL, MEASUREMENTS), 1.0, 6.0, ((0, 8), (1, 4)), jnp.float32)
    scaled_residual_vector = normal_values(keys[2], (MEMBERSHIP_TOTAL, MEASUREMENTS), 1.0, 6.0, ((0, 8), (1, 4)), jnp.float32)
    lattice_coordinates = jnp.clip(2.0 * jax.random.uniform(keys[3], (2, LATTICE_NODES), jnp.float32) ** levels(keys[3], (2, LATTICE_NODES), ((1, 4),), -0.2, 0.2), 0.0, 2.0)
    measurement_coordinates = jnp.clip(jax.random.uniform(keys[4], (2, MEASUREMENTS), jnp.float32, 0.0, 2.0), 0.0, 2.0)
    neighbour_block_totals = draw_neighbour_block_totals(jax.random.fold_in(keys[7], 71), 0)
    neighbour_block_numbers = draw_neighbour_block_numbers(jax.random.fold_in(keys[7], 71), 0)
    return {"prior_matrix": prior_matrix, "prior_at_measurements": prior_at_measurements, "scaled_residual_vector": scaled_residual_vector, "lattice_coordinates": lattice_coordinates, "measurement_coordinates": measurement_coordinates, "neighbour_block_totals": neighbour_block_totals, "neighbour_block_numbers": neighbour_block_numbers}


exact_dot = lax.Precision.HIGHEST

def gaspari_cohn(scaled):
    near_part = scaled * scaled * (scaled * (scaled * (-0.25 * scaled + 0.5) + 0.625) - 5.0 / 3.0) + 1.0
    safe_scaled = jnp.maximum(scaled, 1.0)
    far_part = safe_scaled * (safe_scaled * (safe_scaled * (safe_scaled * (safe_scaled / 12.0 - 0.5) + 0.625) + 5.0 / 3.0) - 5.0) + 4.0 - 2.0 / (3.0 * safe_scaled)
    return jnp.where(scaled <= 1.0, near_part, jnp.where(scaled <= 2.0, far_part, jnp.zeros_like(scaled)))

def taper_tile(grid_xy, obs_xy):
    delta_x = grid_xy[0][:, None] - obs_xy[0][None, :]
    delta_y = grid_xy[1][:, None] - obs_xy[1][None, :]
    distance = jnp.sqrt(delta_x * delta_x + delta_y * delta_y)
    return gaspari_cohn(distance)

def pair_term(lattice_deviation, obs_tile, innov_tile, taper, realization_vectors):
    covariance = lax.dot_general(lattice_deviation, obs_tile, (((0,), (0,)), ((), ())), precision=exact_dot, preferred_element_type=jnp.float32) / (realization_vectors - 1.0)
    weighted = taper * covariance
    return lax.dot_general(innov_tile, weighted, (((1,), (1,)), ((), ())), precision=exact_dot, preferred_element_type=jnp.float32)

def reference(prior_matrix, prior_at_measurements, scaled_residual_vector, lattice_coordinates, measurement_coordinates, neighbour_block_totals, neighbour_block_numbers):
    realization_vectors = prior_matrix.shape[0]
    prior_deviation = prior_matrix - lax.optimization_barrier(jnp.mean(prior_matrix, axis=0, keepdims=True))
    measured_deviation = prior_at_measurements - lax.optimization_barrier(jnp.mean(prior_at_measurements, axis=0, keepdims=True))
    margin = EDGE * OBS_TILE
    padded_anom = jnp.pad(measured_deviation, ((0, 0), (margin, margin)))
    padded_innov = jnp.pad(scaled_residual_vector, ((0, 0), (margin, margin)))
    padded_xy = jnp.pad(measurement_coordinates, ((0, 0), (margin, margin)))

    def one_tile(tile_id):
        slab_index = tile_id // TILES_SLAB
        starting_node = tile_id * BLOCK_NODES
        lattice_deviation = lax.dynamic_slice_in_dim(prior_deviation, starting_node, BLOCK_NODES, 1)
        grid_xy = lax.dynamic_slice_in_dim(lattice_coordinates, starting_node, BLOCK_NODES, 1)

        def add_pair(position, summed):
            ext_id = neighbour_block_numbers[tile_id, position]
            column = ((slab_index * OBS_SLAB + ext_id) * OBS_TILE).astype(jnp.int32)
            obs_tile = lax.dynamic_slice_in_dim(padded_anom, column, OBS_TILE, 1)
            innov_tile = lax.dynamic_slice_in_dim(padded_innov, column, OBS_TILE, 1)
            obs_xy = lax.dynamic_slice_in_dim(padded_xy, column, OBS_TILE, 1)
            taper = taper_tile(grid_xy, obs_xy)
            return summed + pair_term(lattice_deviation, obs_tile, innov_tile, taper, realization_vectors)
        empty = jnp.zeros((realization_vectors, BLOCK_NODES), jnp.float32)
        return lax.fori_loop(0, neighbour_block_totals[tile_id], add_pair, empty)
    increments = lax.map(one_tile, jnp.arange(GRID_TILES, dtype=jnp.int32))
    posterior_correction = jnp.transpose(increments, (1, 0, 2)).reshape(realization_vectors, GRID_TILES * BLOCK_NODES)
    return prior_matrix + posterior_correction
```

```python
import functools

import jax
import jax.numpy as jnp
from jax import lax
from jax.experimental import pallas as pl
from jax.experimental.pallas import tpu as pltpu
from jax.sharding import PartitionSpec as P

TILE = 128
EDGE = 2
GROUP = 2


def with_halo(block, axis, dim, width):
    count = lax.axis_size(axis)
    forward = [(i, i + 1) for i in range(count - 1)]
    backward = [(target, source) for source, target in forward]
    low = lax.ppermute(
        lax.slice_in_dim(block, block.shape[dim] - width, None, axis=dim), axis, forward
    )
    high = lax.ppermute(lax.slice_in_dim(block, 0, width, axis=dim), axis, backward)
    return jnp.concatenate([low, block, high], axis=dim)


def split(x):
    high = x.astype(jnp.bfloat16)
    low = (x - high.astype(jnp.float32)).astype(jnp.bfloat16)
    return high, low


def taper_of(gx, gy, ox, oy):
    dx = ox - gx
    dy = oy - gy
    d2 = dx * dx + dy * dy
    inv = lax.rsqrt(jnp.maximum(d2, 1e-30))
    z = d2 * inv
    a = 0.5 * d2 - 5.0 / 3.0
    near = d2 * (z * (0.625 - 0.25 * d2) + a) + 1.0
    far = d2 * (z * (0.625 + d2 * (1.0 / 12.0)) - a) + (4.0 - 5.0 * z) - (2.0 / 3.0) * inv
    return jnp.where(d2 <= 1.0, near, jnp.where(d2 <= 4.0, far, 0.0))


def dot(a, b):
    return lax.dot_general(a, b, (((1,), (0,)), ((), ())), preferred_element_type=jnp.float32)


def analyse_kernel(
    totals, numbers, fore, obs, innov, gxy, oxy, out, pair_tile, pair_obs, ff, ot, rr, ox, oy, held
):
    slots = totals.shape[0]
    members = fore.shape[0]
    obs_tiles = obs.shape[1] // TILE
    scale = 1.0 / (members - 1.0)

    for lead in range(GROUP):
        pair_tile[lead] = slots
        pair_obs[lead] = 0

    def fill(slot, place):
        count = totals[slot]

        def one(p, carry):
            pair_tile[place + p] = slot
            pair_obs[place + p] = numbers[slot, p]
            return carry

        lax.fori_loop(0, count, one, 0)
        return place + count

    end = lax.fori_loop(0, slots, fill, jnp.int32(GROUP))
    for tail in range(GROUP):
        pair_tile[end + tail] = slots
        pair_obs[end + tail] = 0
    groups = (end - GROUP + GROUP - 1) // GROUP

    def prepare_obs(q, carry):
        columns = pl.ds(pl.multiple_of(q * TILE, TILE), TILE)
        values = obs[:, columns]
        values = values - jnp.mean(values, axis=0, keepdims=True)
        high, low = split(values.T)
        ot[q, :TILE, :] = high
        ot[q, TILE:, :] = low
        high, low = split(innov[:, columns])
        rr[q, :, :TILE] = high
        rr[q, :, TILE:] = low
        ox[q] = jnp.broadcast_to(oxy[0:1, columns], (TILE, TILE)).T
        oy[q] = jnp.broadcast_to(oxy[1:2, columns], (TILE, TILE)).T
        return carry

    lax.fori_loop(0, obs_tiles, prepare_obs, 0)

    def prepare_fore(slot, carry):
        columns = pl.ds(pl.multiple_of(slot * TILE, TILE), TILE)
        values = fore[:, columns]
        values = (values - jnp.mean(values, axis=0, keepdims=True)) * scale
        high, low = split(values)
        ff[slot, :, :TILE] = high
        ff[slot, :, TILE:] = low
        out[:, columns] = jnp.zeros((members, TILE), jnp.float32)
        return carry

    lax.fori_loop(0, slots, prepare_fore, 0)
    held[...] = jnp.zeros_like(held)

    def spend(group):
        terms = []
        for k in range(GROUP):
            q = pair_obs[group * GROUP + k]
            weights = held[k]
            both = dot(rr[q], jnp.concatenate([weights, weights], axis=0))
            terms.append(both[:, :TILE] + both[:, TILE:])
        return terms

    def store(group, terms):
        for k in range(GROUP):
            slot = jnp.minimum(pair_tile[group * GROUP + k], slots - 1)
            columns = pl.ds(pl.multiple_of(slot * TILE, TILE), TILE)
            out[:, columns] += terms[k]

    def body(group, carry):
        terms = spend(group)
        made = []
        for k in range(GROUP):
            place = (group + 1) * GROUP + k
            listed = pair_tile[place]
            slot = jnp.minimum(listed, slots - 1)
            q = pair_obs[place]
            columns = pl.ds(pl.multiple_of(slot * TILE, TILE), TILE)
            away = jnp.where(listed < slots, 0.0, 64.0)
            taper = taper_of(gxy[0:1, columns] + away, gxy[1:2, columns], ox[q], oy[q])
            four = dot(ot[q], ff[slot])
            covariance = four[:TILE, :TILE] + (four[:TILE, TILE:] + four[TILE:, :TILE])
            high, low = split(taper * covariance)
            made.append((high, low))
        for k in range(GROUP):
            held[k, :, :TILE] = made[k][0]
            held[k, :, TILE:] = made[k][1]
        store(group, terms)
        return carry

    lax.fori_loop(0, groups, body, 0)
    store(groups, spend(groups))


def analyse(totals, numbers, fore, obs, innov, gxy, oxy):
    slots, most = numbers.shape
    members, width = fore.shape
    obs_tiles = obs.shape[1] // TILE
    room = slots * most + 2 * GROUP
    smem = pl.BlockSpec(memory_space=pltpu.SMEM)
    vmem = pl.BlockSpec(memory_space=pltpu.VMEM)
    return pl.pallas_call(
        analyse_kernel,
        out_shape=jax.ShapeDtypeStruct((members, width), jnp.float32),
        in_specs=[smem, smem, vmem, vmem, vmem, vmem, vmem],
        out_specs=vmem,
        scratch_shapes=[
            pltpu.SMEM((room,), jnp.int32),
            pltpu.SMEM((room,), jnp.int32),
            pltpu.VMEM((slots, members, 2 * TILE), jnp.bfloat16),
            pltpu.VMEM((obs_tiles, 2 * TILE, members), jnp.bfloat16),
            pltpu.VMEM((obs_tiles, members, 2 * TILE), jnp.bfloat16),
            pltpu.VMEM((obs_tiles, TILE, TILE), jnp.float32),
            pltpu.VMEM((obs_tiles, TILE, TILE), jnp.float32),
            pltpu.VMEM((GROUP, TILE, 2 * TILE), jnp.bfloat16),
        ],
        compiler_params=pltpu.CompilerParams(vmem_limit_bytes=48 * 1024 * 1024),
    )(totals, numbers, fore, obs, innov, gxy, oxy)


def per_device(
    prior_matrix,
    prior_at_measurements,
    scaled_residual_vector,
    lattice_coordinates,
    measurement_coordinates,
    neighbour_block_totals,
    neighbour_block_numbers,
):
    regions = lax.axis_size("region")
    region = lax.axis_index("region")
    slab = lax.axis_index("slab")
    mine, points = prior_matrix.shape
    members = mine * regions
    tiles = neighbour_block_totals.shape[0]
    slots = tiles // regions
    margin = EDGE * TILE
    slab_obs = prior_at_measurements.shape[1]

    piled = jnp.stack((prior_at_measurements, scaled_residual_vector))
    obs_whole = lax.all_gather(with_halo(piled, "slab", 2, margin), "region", axis=1, tiled=True)

    blocks = prior_matrix.reshape(mine, slots, regions, TILE).transpose(2, 0, 1, 3)
    owned = lax.all_to_all(
        blocks.reshape(regions, mine, slots * TILE), "region", split_axis=0, concat_axis=0, tiled=True
    ).reshape(members, slots * TILE)

    def own(x, axis):
        shape = x.shape[:axis] + (slots, regions) + x.shape[axis + 1 :]
        return lax.dynamic_index_in_dim(x.reshape(shape), region, axis + 1, False)

    totals = own(neighbour_block_totals, 0)
    numbers = own(neighbour_block_numbers, 0)
    gxy = own(lattice_coordinates.reshape(2, tiles, TILE), 1).reshape(2, slots * TILE)
    padded = jnp.pad(measurement_coordinates, ((0, 0), (margin, margin)))
    oxy = lax.dynamic_slice_in_dim(padded, slab * slab_obs, slab_obs + 2 * margin, 1)

    increment = analyse(totals, numbers, owned, obs_whole[0], obs_whole[1], gxy, oxy)

    returned = lax.all_to_all(
        increment.reshape(regions, mine, slots * TILE), "region", split_axis=0, concat_axis=0, tiled=True
    )
    back = returned.reshape(regions, mine, slots, TILE).transpose(1, 2, 0, 3)
    return prior_matrix + back.reshape(mine, points)


def solution(mesh):
    in_specs = (
        P("region", "slab"),
        P("region", "slab"),
        P("region", "slab"),
        P(None, "slab"),
        P(),
        P("slab"),
        P("slab", None),
    )
    return jax.shard_map(
        per_device, mesh=mesh, in_specs=in_specs, out_specs=P("region", "slab"), check_vma=False
    )
```

```python
import functools

import jax
import jax.numpy as jnp
from jax import lax
from jax.experimental import pallas as pl
from jax.experimental.pallas import tpu as pltpu
from jax.sharding import PartitionSpec as P

TILE = 128
EDGE = 2
GROUP = 2
MESH = pl.DeviceIdType.MESH


def flip(index, bits):
    step = 1
    while step <= bits:
        if bits & step:
            index = index + step - 2 * step * ((index // step) % 2)
        step *= 2
    return index


def push(src, dst, send, recv, slab, region):
    copy = pltpu.make_async_remote_copy(
        src_ref=src,
        dst_ref=dst,
        send_sem=send,
        recv_sem=recv,
        device_id=(slab, region),
        device_id_type=MESH,
    )
    copy.start()
    return copy


def collect_kernel(
    n,
    slabs,
    prior,
    obs,
    res,
    fore,
    obs_all,
    res_all,
    own_sem,
    fore_send,
    fore_recv,
    near_send,
    near_recv,
    pass_send,
    edge_send,
    edge_recv,
):
    slab = lax.axis_index("slab")
    region = lax.axis_index("region")
    mine, points = obs.shape
    groups = prior.shape[0]
    margin = EDGE * TILE
    sources = (obs, res)
    targets = (obs_all, res_all)
    above = slab < slabs - 1
    below = slab > 0

    def rows(owner):
        return pl.ds(pl.multiple_of(owner * mine, 8), mine)

    def fore_rows(owner):
        return pl.ds(owner * groups, groups)

    middle = pl.ds(margin, points)
    low = pl.ds(0, margin)
    high = pl.ds(margin + points, margin)

    barrier = pltpu.get_barrier_semaphore()
    for k in range(1, n):
        pl.semaphore_signal(
            barrier, inc=1, device_id=(slab, flip(region, k)), device_id_type=MESH
        )

    for exists, other in ((above, slab + 1), (below, slab - 1)):

        @pl.when(exists)
        def _(other=other):
            for k in (0, 1):
                pl.semaphore_signal(
                    barrier, inc=1, device_id=(other, flip(region, k)), device_id_type=MESH
                )

    beside = above.astype(jnp.int32) + below.astype(jnp.int32)
    pl.semaphore_wait(barrier, n - 1 + 2 * beside)

    def edge_copies(k, side, other, act):
        block = rows(flip(region, k))
        for a in range(2):
            if k == 0:
                src = sources[a].at[:, pl.ds(points - margin, margin) if side == 0 else low]
            else:
                first = points if side == 0 else margin
                src = targets[a].at[block, pl.ds(first, margin)]
            for core in range(2):
                copy = pltpu.make_async_remote_copy(
                    src_ref=src,
                    dst_ref=targets[a].at[block, low if side == 0 else high],
                    send_sem=edge_send.at[side, a, k + core],
                    recv_sem=edge_recv.at[side, a, k + core],
                    device_id=(other, flip(region, core)),
                    device_id_type=MESH,
                )
                act(copy)

    def send_edges(k):
        for side, exists, other in ((0, above, slab + 1), (1, below, slab - 1)):

            @pl.when(exists)
            def _(side=side, other=other):
                edge_copies(k, side, other, lambda copy: copy.start())

    sent = []
    for k in [*range(2, n, 2), 1]:
        for a in range(2):
            sent.append(
                push(
                    sources[a],
                    targets[a].at[rows(region), middle],
                    near_send.at[a, k],
                    near_recv.at[a, k],
                    slab,
                    flip(region, k),
                )
            )
    send_edges(0)
    own = [
        pltpu.make_async_copy(sources[a], targets[a].at[rows(region), middle], own_sem.at[a])
        for a in range(2)
    ]
    own.append(pltpu.make_async_copy(prior.at[:, :, region], fore.at[fore_rows(region)], own_sem.at[2]))
    for k in [*range(2, n), 1]:
        sent.append(
            push(
                prior.at[:, :, flip(region, k)],
                fore.at[fore_rows(region)],
                fore_send.at[k],
                fore_recv.at[k],
                slab,
                flip(region, k),
            )
        )
    for copy in own:
        copy.start()

    def near_wait(a, k):
        place = targets[a].at[rows(flip(region, k)), middle]
        pltpu.make_async_copy(place, place, near_recv.at[a, k]).wait()

    for k in range(2, n, 2):
        for a in range(2):
            near_wait(a, k)
            place = targets[a].at[rows(flip(region, k)), middle]
            sent.append(
                push(
                    place, place, pass_send.at[a, k], near_recv.at[a, k + 1], slab, flip(region, 1)
                )
            )
        send_edges(k)

    for k in range(1, n, 2):
        for a in range(2):
            near_wait(a, k)
    for k in range(1, n):
        place = fore.at[fore_rows(flip(region, k))]
        pltpu.make_async_copy(place, place, fore_recv.at[k]).wait()
    for side, comes in ((0, below), (1, above)):

        @pl.when(comes)
        def _(side=side):
            for k in range(n):
                for a in range(2):
                    place = targets[a].at[rows(flip(region, k)), low if side == 0 else high]
                    pltpu.make_async_copy(place, place, edge_recv.at[side, a, k]).wait()

    for side, exists, other in ((0, above, slab + 1), (1, below, slab - 1)):

        @pl.when(exists)
        def _(side=side, other=other):
            for k in range(0, n, 2):
                edge_copies(k, side, other, lambda copy: copy.wait_send())

    for copy in sent:
        copy.wait_send()
    for copy in own:
        copy.wait()


def collect(n, slabs, prior, obs, res):
    groups, slots = prior.shape[:2]
    mine, points = obs.shape
    wide = jax.ShapeDtypeStruct((mine * n, points + 2 * EDGE * TILE), jnp.float32)
    hbm = pl.BlockSpec(memory_space=pl.ANY)
    dma = pltpu.SemaphoreType.DMA
    return pl.pallas_call(
        functools.partial(collect_kernel, n, slabs),
        out_shape=(jax.ShapeDtypeStruct((groups * n, slots, 8, TILE), jnp.float32), wide, wide),
        in_specs=[hbm] * 3,
        out_specs=(hbm,) * 3,
        scratch_shapes=[
            dma((3,)),
            dma((n,)),
            dma((n,)),
            dma((2, n)),
            dma((2, n)),
            dma((2, n)),
            dma((2, 2, n)),
            dma((2, 2, n)),
        ],
        compiler_params=pltpu.CompilerParams(collective_id=0, has_side_effects=True),
    )(prior, obs, res)


def return_kernel(n, increment, back, own_sem, send, recv):
    slab = lax.axis_index("slab")
    region = lax.axis_index("region")
    groups = back.shape[0]
    barrier = pltpu.get_barrier_semaphore()
    for k in range(1, n):
        pl.semaphore_signal(
            barrier, inc=1, device_id=(slab, flip(region, k)), device_id_type=MESH
        )
    pl.semaphore_wait(barrier, n - 1)
    sent = []
    for k in [*range(2, n), 1]:
        other = flip(region, k)
        sent.append(
            push(
                increment.at[pl.ds(other * groups, groups)],
                back.at[:, :, region],
                send.at[k],
                recv.at[k],
                slab,
                other,
            )
        )
    own = pltpu.make_async_copy(
        increment.at[pl.ds(region * groups, groups)], back.at[:, :, region], own_sem
    )
    own.start()
    for k in range(1, n):
        place = back.at[:, :, flip(region, k)]
        pltpu.make_async_copy(place, place, recv.at[k]).wait()
    for copy in sent:
        copy.wait_send()
    own.wait()


def send_back(n, increment):
    total, slots = increment.shape[:2]
    hbm = pl.BlockSpec(memory_space=pl.ANY)
    dma = pltpu.SemaphoreType.DMA
    return pl.pallas_call(
        functools.partial(return_kernel, n),
        out_shape=jax.ShapeDtypeStruct((total // n, slots, n, 8, TILE), jnp.float32),
        in_specs=[hbm],
        out_specs=hbm,
        scratch_shapes=[dma, dma((n,)), dma((n,))],
        compiler_params=pltpu.CompilerParams(collective_id=1, has_side_effects=True),
    )(increment)


def split(x):
    high = x.astype(jnp.bfloat16)
    low = (x - high.astype(jnp.float32)).astype(jnp.bfloat16)
    return high, low


def taper_of(gx, gy, ox, oy):
    dx = ox - gx
    dy = oy - gy
    d2 = dx * dx + dy * dy
    inv = lax.rsqrt(jnp.maximum(d2, 1e-30))
    z = d2 * inv
    a = 0.5 * d2 - 5.0 / 3.0
    near = d2 * (z * (0.625 - 0.25 * d2) + a) + 1.0
    far = d2 * (z * (0.625 + d2 * (1.0 / 12.0)) - a) + (4.0 - 5.0 * z) - (2.0 / 3.0) * inv
    return jnp.where(d2 <= 1.0, near, jnp.where(d2 <= 4.0, far, 0.0))


def dot(a, b):
    return lax.dot_general(a, b, (((1,), (0,)), ((), ())), preferred_element_type=jnp.float32)


def analyse_kernel(
    totals, numbers, fore, obs, innov, gxy, oxy, out, pair_tile, pair_obs, ff, ot, rr, ox, oy, held
):
    slots = totals.shape[0]
    members = fore.shape[0]
    obs_tiles = obs.shape[1] // TILE
    scale = 1.0 / (members - 1.0)

    for lead in range(GROUP):
        pair_tile[lead] = slots
        pair_obs[lead] = EDGE

    def fill(slot, place):
        count = totals[slot]

        def one(p, carry):
            pair_tile[place + p] = slot
            pair_obs[place + p] = numbers[slot, p]
            return carry

        lax.fori_loop(0, count, one, 0)
        return place + count

    end = lax.fori_loop(0, slots, fill, jnp.int32(GROUP))
    for tail in range(GROUP):
        pair_tile[end + tail] = slots
        pair_obs[end + tail] = EDGE
    groups = (end - GROUP + GROUP - 1) // GROUP

    def prepare_obs(q, carry):
        columns = pl.ds(pl.multiple_of(q * TILE, TILE), TILE)
        values = obs[:, columns]
        values = values - jnp.mean(values, axis=0, keepdims=True)
        high, low = split(values.T)
        ot[q, :TILE, :] = high
        ot[q, TILE:, :] = low
        high, low = split(innov[:, columns])
        rr[q, :, :TILE] = high
        rr[q, :, TILE:] = low
        ox[q] = jnp.broadcast_to(oxy[0:1, columns], (TILE, TILE)).T
        oy[q] = jnp.broadcast_to(oxy[1:2, columns], (TILE, TILE)).T
        return carry

    lax.fori_loop(0, obs_tiles, prepare_obs, 0)

    def prepare_fore(slot, carry):
        columns = pl.ds(pl.multiple_of(slot * TILE, TILE), TILE)
        values = fore[:, columns]
        values = (values - jnp.mean(values, axis=0, keepdims=True)) * scale
        high, low = split(values)
        ff[slot, :, :TILE] = high
        ff[slot, :, TILE:] = low
        out[:, columns] = jnp.zeros((members, TILE), jnp.float32)
        return carry

    lax.fori_loop(0, slots, prepare_fore, 0)
    held[...] = jnp.zeros_like(held)

    def spend(group):
        terms = []
        for k in range(GROUP):
            q = pair_obs[group * GROUP + k]
            weights = held[k]
            both = dot(rr[q], jnp.concatenate([weights, weights], axis=0))
            terms.append(both[:, :TILE] + both[:, TILE:])
        return terms

    def store(group, terms):
        for k in range(GROUP):
            slot = jnp.minimum(pair_tile[group * GROUP + k], slots - 1)
            columns = pl.ds(pl.multiple_of(slot * TILE, TILE), TILE)
            out[:, columns] += terms[k]

    def body(group, carry):
        terms = spend(group)
        made = []
        for k in range(GROUP):
            place = (group + 1) * GROUP + k
            listed = pair_tile[place]
            slot = jnp.minimum(listed, slots - 1)
            q = pair_obs[place]
            columns = pl.ds(pl.multiple_of(slot * TILE, TILE), TILE)
            away = jnp.where(listed < slots, 0.0, 64.0)
            taper = taper_of(gxy[0:1, columns] + away, gxy[1:2, columns], ox[q], oy[q])
            four = dot(ot[q], ff[slot])
            covariance = four[:TILE, :TILE] + (four[:TILE, TILE:] + four[TILE:, :TILE])
            high, low = split(taper * covariance)
            made.append((high, low))
        for k in range(GROUP):
            held[k, :, :TILE] = made[k][0]
            held[k, :, TILE:] = made[k][1]
        store(group, terms)
        return carry

    lax.fori_loop(0, groups, body, 0)
    store(groups, spend(groups))


def analyse(totals, numbers, fore, obs, innov, gxy, oxy):
    slots, most = numbers.shape
    members, width = fore.shape
    obs_tiles = obs.shape[1] // TILE
    room = slots * most + 2 * GROUP
    smem = pl.BlockSpec(memory_space=pltpu.SMEM)
    vmem = pl.BlockSpec(memory_space=pltpu.VMEM)
    return pl.pallas_call(
        analyse_kernel,
        out_shape=jax.ShapeDtypeStruct((members, width), jnp.float32),
        in_specs=[smem, smem, vmem, vmem, vmem, vmem, vmem],
        out_specs=vmem,
        scratch_shapes=[
            pltpu.SMEM((room,), jnp.int32),
            pltpu.SMEM((room,), jnp.int32),
            pltpu.VMEM((slots, members, 2 * TILE), jnp.bfloat16),
            pltpu.VMEM((obs_tiles, 2 * TILE, members), jnp.bfloat16),
            pltpu.VMEM((obs_tiles, members, 2 * TILE), jnp.bfloat16),
            pltpu.VMEM((obs_tiles, TILE, TILE), jnp.float32),
            pltpu.VMEM((obs_tiles, TILE, TILE), jnp.float32),
            pltpu.VMEM((GROUP, TILE, 2 * TILE), jnp.bfloat16),
        ],
        compiler_params=pltpu.CompilerParams(vmem_limit_bytes=48 * 1024 * 1024),
    )(totals, numbers, fore, obs, innov, gxy, oxy)


def per_device(
    prior_matrix,
    prior_at_measurements,
    scaled_residual_vector,
    lattice_coordinates,
    measurement_coordinates,
    neighbour_block_totals,
    neighbour_block_numbers,
):
    regions = lax.axis_size("region")
    region = lax.axis_index("region")
    slab = lax.axis_index("slab")
    mine, points = prior_matrix.shape
    members = mine * regions
    tiles = neighbour_block_totals.shape[0]
    slots = tiles // regions
    margin = EDGE * TILE
    slab_obs = prior_at_measurements.shape[1]

    blocks = prior_matrix.reshape(mine // 8, 8, slots, regions, TILE).transpose(0, 2, 3, 1, 4)
    fore, obs_all, res_all = collect(
        regions, lax.axis_size("slab"), blocks, prior_at_measurements, scaled_residual_vector
    )
    owned = fore.transpose(0, 2, 1, 3).reshape(members, slots * TILE)

    def own(x, axis):
        shape = x.shape[:axis] + (slots, regions) + x.shape[axis + 1 :]
        return lax.dynamic_index_in_dim(x.reshape(shape), region, axis + 1, False)

    totals = own(neighbour_block_totals, 0)
    numbers = own(neighbour_block_numbers, 0)
    gxy = own(lattice_coordinates.reshape(2, tiles, TILE), 1).reshape(2, slots * TILE)
    padded = jnp.pad(measurement_coordinates, ((0, 0), (margin, margin)))
    oxy = lax.dynamic_slice_in_dim(padded, slab * slab_obs, slab_obs + 2 * margin, 1)

    increment = analyse(totals, numbers, owned, obs_all, res_all, gxy, oxy)
    cut = increment.reshape(members // 8, 8, slots, TILE).transpose(0, 2, 1, 3)
    back = send_back(regions, cut)
    return prior_matrix + back.transpose(0, 3, 1, 2, 4).reshape(mine, points)


def solution(mesh):
    in_specs = (
        P("region", "slab"),
        P("region", "slab"),
        P("region", "slab"),
        P(None, "slab"),
        P(),
        P("slab"),
        P("slab", None),
    )
    return jax.shard_map(
        per_device, mesh=mesh, in_specs=in_specs, out_specs=P("region", "slab"), check_vma=False
    )
```

```python
import functools

import jax
import jax.numpy as jnp
from jax import lax
from jax.experimental import pallas as pl
from jax.experimental.pallas import tpu as pltpu
from jax.sharding import PartitionSpec as P

TILE = 128
EDGE = 2
GROUP = 4
MESH = pl.DeviceIdType.MESH


def flip(index, bits):
    step = 1
    while step <= bits:
        if bits & step:
            index = index + step - 2 * step * ((index // step) % 2)
        step *= 2
    return index


def push(src, dst, send, recv, slab, region):
    copy = pltpu.make_async_remote_copy(
        src_ref=src,
        dst_ref=dst,
        send_sem=send,
        recv_sem=recv,
        device_id=(slab, region),
        device_id_type=MESH,
    )
    copy.start()
    return copy


def collect_kernel(
    n,
    slabs,
    prior,
    obs,
    res,
    oxy,
    fore,
    ot,
    rr,
    ox,
    oy,
    obs_all,
    res_all,
    own_sem,
    fore_send,
    fore_recv,
    near_send,
    near_recv,
    edge_send,
    edge_recv,
):
    slab = lax.axis_index("slab")
    region = lax.axis_index("region")
    mine, points = obs.shape
    groups = prior.shape[0]
    margin = EDGE * TILE
    sources = (obs, res)
    targets = (obs_all, res_all)
    above = slab < slabs - 1
    below = slab > 0

    def rows(owner):
        return pl.ds(pl.multiple_of(owner * mine, 8), mine)

    def fore_rows(owner):
        return pl.ds(owner * groups, groups)

    middle = pl.ds(margin, points)
    low = pl.ds(0, margin)
    high = pl.ds(margin + points, margin)

    barrier = pltpu.get_barrier_semaphore()
    for k in range(1, n):
        pl.semaphore_signal(
            barrier, inc=1, device_id=(slab, flip(region, k)), device_id_type=MESH
        )

    for exists, other in ((above, slab + 1), (below, slab - 1)):

        @pl.when(exists)
        def _(other=other):
            for k in (0, 1):
                pl.semaphore_signal(
                    barrier, inc=1, device_id=(other, flip(region, k)), device_id_type=MESH
                )

    beside = above.astype(jnp.int32) + below.astype(jnp.int32)
    pl.semaphore_wait(barrier, n - 1 + 2 * beside)

    def edge_copies(k, side, other, act):
        block = rows(flip(region, k))
        for a in range(2):
            if k == 0:
                src = sources[a].at[:, pl.ds(points - margin, margin) if side == 0 else low]
            else:
                first = points if side == 0 else margin
                src = targets[a].at[block, pl.ds(first, margin)]
            for core in range(2):
                copy = pltpu.make_async_remote_copy(
                    src_ref=src,
                    dst_ref=targets[a].at[block, low if side == 0 else high],
                    send_sem=edge_send.at[side, a, k + core],
                    recv_sem=edge_recv.at[side, a, k + core],
                    device_id=(other, flip(region, core)),
                    device_id_type=MESH,
                )
                act(copy)

    def send_edges(k):
        for side, exists, other in ((0, above, slab + 1), (1, below, slab - 1)):

            @pl.when(exists)
            def _(side=side, other=other):
                edge_copies(k, side, other, lambda copy: copy.start())

    sent = []
    bits = [1 << b for b in range(1, n.bit_length() - 1)]

    def forward(k):
        for a in range(2):
            place = targets[a].at[rows(flip(region, k)), middle]
            src = sources[a] if k == 0 else place
            for bit in bits:
                to = k | bit
                last = [b for b in bits if b & to][-1 if a == 0 else 0]
                if k & bit or last != bit:
                    continue
                sent.append(
                    push(
                        src,
                        place,
                        near_send.at[a, to],
                        near_recv.at[a, to],
                        slab,
                        flip(region, bit),
                    )
                )
            sent.append(
                push(src, place, near_send.at[a, k + 1], near_recv.at[a, k + 1], slab, flip(region, 1))
            )

    def near_wait(a, k):
        place = targets[a].at[rows(flip(region, k)), middle]
        pltpu.make_async_copy(place, place, near_recv.at[a, k]).wait()

    def send_fore():
        for k in [*range(2, n), 1]:
            sent.append(
                push(
                    prior.at[:, :, flip(region, k)],
                    fore.at[fore_rows(region)],
                    fore_send.at[k],
                    fore_recv.at[k],
                    slab,
                    flip(region, k),
                )
            )

    forward(0)
    send_edges(0)
    own = [
        pltpu.make_async_copy(sources[a], targets[a].at[rows(region), middle], own_sem.at[a])
        for a in range(2)
    ]
    own.append(pltpu.make_async_copy(prior.at[:, :, region], fore.at[fore_rows(region)], own_sem.at[2]))
    for copy in own:
        copy.start()

    even = sorted(range(2, n, 2), key=lambda k: (k.bit_count(), k))
    for k in even:
        for a in range(2):
            near_wait(a, k)
        forward(k)
        if k == bits[-1]:
            send_fore()
        send_edges(k)
    if not bits:
        send_fore()

    for k in range(1, n, 2):
        for a in range(2):
            near_wait(a, k)
    for side, comes in ((0, below), (1, above)):

        @pl.when(comes)
        def _(side=side):
            for k in range(n):
                for a in range(2):
                    place = targets[a].at[rows(flip(region, k)), low if side == 0 else high]
                    pltpu.make_async_copy(place, place, edge_recv.at[side, a, k]).wait()

    for copy in own[:2]:
        copy.wait()

    last_tile = oxy.shape[1] // TILE - 1
    first_tile = slab * (points // TILE) - EDGE

    def prepare(q, carry):
        columns = pl.ds(pl.multiple_of(q * TILE, TILE), TILE)
        values = obs_all[:, columns]
        values = values - jnp.mean(values, axis=0, keepdims=True)
        high, low = split(values.T)
        ot[q, :TILE, :] = high
        ot[q, TILE:, :] = low
        high, low = split(res_all[:, columns])
        rr[q, :, :TILE] = high
        rr[q, :, TILE:] = low
        place = jnp.clip(first_tile + q, 0, last_tile)
        there = pl.ds(pl.multiple_of(place * TILE, TILE), TILE)
        ox[q] = jnp.broadcast_to(oxy[0:1, there], (TILE, TILE)).T
        oy[q] = jnp.broadcast_to(oxy[1:2, there], (TILE, TILE)).T
        return carry

    lax.fori_loop(0, obs_all.shape[1] // TILE, prepare, 0)

    for k in range(1, n):
        place = fore.at[fore_rows(flip(region, k))]
        pltpu.make_async_copy(place, place, fore_recv.at[k]).wait()
    for side, exists, other in ((0, above, slab + 1), (1, below, slab - 1)):

        @pl.when(exists)
        def _(side=side, other=other):
            for k in range(0, n, 2):
                edge_copies(k, side, other, lambda copy: copy.wait_send())

    for copy in sent:
        copy.wait_send()
    own[2].wait()


def collect(n, slabs, prior, obs, res, oxy):
    groups, slots = prior.shape[:2]
    mine, points = obs.shape
    members = mine * n
    wide = pltpu.VMEM((members, points + 2 * EDGE * TILE), jnp.float32)
    obs_tiles = points // TILE + 2 * EDGE
    spread = jax.ShapeDtypeStruct((obs_tiles, TILE, TILE), jnp.float32)
    vmem = pl.BlockSpec(memory_space=pltpu.VMEM)
    hbm = pl.BlockSpec(memory_space=pl.ANY)
    dma = pltpu.SemaphoreType.DMA
    return pl.pallas_call(
        functools.partial(collect_kernel, n, slabs),
        out_shape=(
            jax.ShapeDtypeStruct((groups * n, slots, 8, TILE), jnp.float32),
            jax.ShapeDtypeStruct((obs_tiles, 2 * TILE, members), jnp.bfloat16),
            jax.ShapeDtypeStruct((obs_tiles, members, 2 * TILE), jnp.bfloat16),
            spread,
            spread,
        ),
        in_specs=[hbm, hbm, hbm, vmem],
        out_specs=(hbm, vmem, vmem, vmem, vmem),
        scratch_shapes=[
            wide,
            wide,
            dma((3,)),
            dma((n,)),
            dma((n,)),
            dma((2, n)),
            dma((2, n)),
            dma((2, 2, n)),
            dma((2, 2, n)),
        ],
        compiler_params=pltpu.CompilerParams(
            collective_id=0, has_side_effects=True, vmem_limit_bytes=32 * 1024 * 1024
        ),
    )(prior, obs, res, oxy)


def return_kernel(n, increment, back, own_sem, send, recv):
    slab = lax.axis_index("slab")
    region = lax.axis_index("region")
    groups = back.shape[0]
    barrier = pltpu.get_barrier_semaphore()
    for k in range(1, n):
        pl.semaphore_signal(
            barrier, inc=1, device_id=(slab, flip(region, k)), device_id_type=MESH
        )
    pl.semaphore_wait(barrier, n - 1)
    sent = []
    for k in [*range(2, n), 1]:
        other = flip(region, k)
        sent.append(
            push(
                increment.at[pl.ds(other * groups, groups)],
                back.at[:, :, region],
                send.at[k],
                recv.at[k],
                slab,
                other,
            )
        )
    own = pltpu.make_async_copy(
        increment.at[pl.ds(region * groups, groups)], back.at[:, :, region], own_sem
    )
    own.start()
    for k in range(1, n):
        place = back.at[:, :, flip(region, k)]
        pltpu.make_async_copy(place, place, recv.at[k]).wait()
    for copy in sent:
        copy.wait_send()
    own.wait()


def send_back(n, increment):
    total, slots = increment.shape[:2]
    hbm = pl.BlockSpec(memory_space=pl.ANY)
    dma = pltpu.SemaphoreType.DMA
    return pl.pallas_call(
        functools.partial(return_kernel, n),
        out_shape=jax.ShapeDtypeStruct((total // n, slots, n, 8, TILE), jnp.float32),
        in_specs=[hbm],
        out_specs=hbm,
        scratch_shapes=[dma, dma((n,)), dma((n,))],
        compiler_params=pltpu.CompilerParams(collective_id=1, has_side_effects=True),
    )(increment)


def split(x):
    high = x.astype(jnp.bfloat16)
    low = (x - high.astype(jnp.float32)).astype(jnp.bfloat16)
    return high, low


def taper_of(gx, gy, ox, oy):
    dx = ox - gx
    dy = oy - gy
    d2 = dx * dx + dy * dy
    inv = lax.rsqrt(jnp.maximum(d2, 1e-30))
    z = d2 * inv
    a = 0.5 * d2 - 5.0 / 3.0
    near = d2 * (z * (0.625 - 0.25 * d2) + a) + 1.0
    far = d2 * (z * (0.625 + d2 * (1.0 / 12.0)) - a) + (4.0 - 5.0 * z) - (2.0 / 3.0) * inv
    return jnp.where(d2 <= 1.0, near, jnp.where(d2 <= 4.0, far, 0.0))


def dot(a, b):
    return lax.dot_general(a, b, (((1,), (0,)), ((), ())), preferred_element_type=jnp.float32)


def analyse_kernel(
    regions, totals, numbers, fore, ot, rr, ox, oy, gxy, out, pair_tile, pair_obs, ff, held
):
    region = lax.axis_index("region")
    slots = fore.shape[1] // TILE
    members = fore.shape[0]
    scale = 1.0 / (members - 1.0)

    for lead in range(GROUP):
        pair_tile[lead] = slots
        pair_obs[lead] = EDGE

    def fill(slot, place):
        tile = slot * regions + region
        count = totals[tile]

        def one(p, carry):
            pair_tile[place + p] = slot
            pair_obs[place + p] = numbers[p, tile]
            return carry

        lax.fori_loop(0, count, one, 0)
        return place + count

    end = lax.fori_loop(0, slots, fill, jnp.int32(GROUP))
    for tail in range(GROUP):
        pair_tile[end + tail] = slots
        pair_obs[end + tail] = EDGE
    groups = (end - GROUP + GROUP - 1) // GROUP

    def prepare_fore(slot, carry):
        columns = pl.ds(pl.multiple_of(slot * TILE, TILE), TILE)
        values = fore[:, columns]
        values = (values - jnp.mean(values, axis=0, keepdims=True)) * scale
        high, low = split(values)
        ff[slot, :, :TILE] = high
        ff[slot, :, TILE:] = low
        out[:, columns] = jnp.zeros((members, TILE), jnp.float32)
        return carry

    lax.fori_loop(0, slots, prepare_fore, 0)
    held[...] = jnp.zeros_like(held)

    def spend(group):
        terms = []
        for k in range(GROUP):
            q = pair_obs[group * GROUP + k]
            weights = held[k]
            both = dot(rr[q], jnp.concatenate([weights, weights], axis=0))
            terms.append(both[:, :TILE] + both[:, TILE:])
        return terms

    def store(group, terms):
        for k in range(GROUP):
            slot = jnp.minimum(pair_tile[group * GROUP + k], slots - 1)
            columns = pl.ds(pl.multiple_of(slot * TILE, TILE), TILE)
            out[:, columns] += terms[k]

    def body(group, carry):
        terms = spend(group)
        made = []
        for k in range(GROUP):
            place = (group + 1) * GROUP + k
            listed = pair_tile[place]
            slot = jnp.minimum(listed, slots - 1)
            q = pair_obs[place]
            tile = slot * regions + region
            columns = pl.ds(pl.multiple_of(tile * TILE, TILE), TILE)
            away = jnp.where(listed < slots, 0.0, 64.0)
            taper = taper_of(gxy[0:1, columns] + away, gxy[1:2, columns], ox[q], oy[q])
            four = dot(ot[q], ff[slot])
            covariance = four[:TILE, :TILE] + (four[:TILE, TILE:] + four[TILE:, :TILE])
            high, low = split(taper * covariance)
            made.append((high, low))
        for k in range(GROUP):
            held[k, :, :TILE] = made[k][0]
            held[k, :, TILE:] = made[k][1]
        store(group, terms)
        return carry

    lax.fori_loop(0, groups, body, 0)
    store(groups, spend(groups))


def analyse(regions, totals, numbers, fore, ot, rr, ox, oy, gxy):
    most = numbers.shape[0]
    members, width = fore.shape
    slots = width // TILE
    room = slots * most + 2 * GROUP
    smem = pl.BlockSpec(memory_space=pltpu.SMEM)
    vmem = pl.BlockSpec(memory_space=pltpu.VMEM)
    return pl.pallas_call(
        functools.partial(analyse_kernel, regions),
        out_shape=jax.ShapeDtypeStruct((members, width), jnp.float32),
        in_specs=[smem, smem, vmem, vmem, vmem, vmem, vmem, vmem],
        out_specs=vmem,
        scratch_shapes=[
            pltpu.SMEM((room,), jnp.int32),
            pltpu.SMEM((room,), jnp.int32),
            pltpu.VMEM((slots, members, 2 * TILE), jnp.bfloat16),
            pltpu.VMEM((GROUP, TILE, 2 * TILE), jnp.bfloat16),
        ],
        compiler_params=pltpu.CompilerParams(vmem_limit_bytes=32 * 1024 * 1024),
    )(totals, numbers, fore, ot, rr, ox, oy, gxy)


def per_device(
    prior_matrix,
    prior_at_measurements,
    scaled_residual_vector,
    lattice_coordinates,
    measurement_coordinates,
    neighbour_block_totals,
    neighbour_block_numbers,
):
    regions = lax.axis_size("region")
    mine, points = prior_matrix.shape
    members = mine * regions
    slots = neighbour_block_totals.shape[0] // regions

    blocks = prior_matrix.reshape(mine // 8, 8, slots, regions, TILE).transpose(0, 2, 3, 1, 4)
    fore, *prepared = collect(
        regions,
        lax.axis_size("slab"),
        blocks,
        prior_at_measurements,
        scaled_residual_vector,
        measurement_coordinates,
    )
    owned = fore.transpose(0, 2, 1, 3).reshape(members, slots * TILE)
    increment = analyse(
        regions,
        neighbour_block_totals,
        neighbour_block_numbers.T,
        owned,
        *prepared,
        lattice_coordinates,
    )
    cut = increment.reshape(members // 8, 8, slots, TILE).transpose(0, 2, 1, 3)
    back = send_back(regions, cut)
    return prior_matrix + back.transpose(0, 3, 1, 2, 4).reshape(mine, points)


def solution(mesh):
    in_specs = (
        P("region", "slab"),
        P("region", "slab"),
        P("region", "slab"),
        P(None, "slab"),
        P(),
        P("slab"),
        P("slab", None),
    )
    return jax.shard_map(
        per_device, mesh=mesh, in_specs=in_specs, out_specs=P("region", "slab"), check_vma=False
    )
```

```python
import functools

import jax
import jax.numpy as jnp
from jax import lax
from jax.experimental import pallas as pl
from jax.experimental.pallas import tpu as pltpu
from jax.sharding import PartitionSpec as P

TILE = 128
EDGE = 2
GROUP = 4
PARTS = 4
MESH = pl.DeviceIdType.MESH


def flip(index, bits):
    step = 1
    while step <= bits:
        if bits & step:
            index = index + step - 2 * step * ((index // step) % 2)
        step *= 2
    return index


def push(src, dst, send, recv, slab, region):
    copy = pltpu.make_async_remote_copy(
        src_ref=src,
        dst_ref=dst,
        send_sem=send,
        recv_sem=recv,
        device_id=(slab, region),
        device_id_type=MESH,
    )
    copy.start()
    return copy


def ensemble_kernel(
    n,
    slabs,
    parts,
    totals,
    numbers,
    prior,
    obs,
    res,
    gxy,
    oxy,
    back,
    fore,
    increment,
    obs_all,
    res_all,
    ot,
    rr,
    ox,
    oy,
    tapers,
    ff,
    held,
    own_sem,
    fore_send,
    fore_recv,
    near_send,
    near_recv,
    edge_send,
    edge_recv,
    back_send,
    back_recv,
):
    slab = lax.axis_index("slab")
    region = lax.axis_index("region")
    mine, points = obs.shape
    groups, slots = prior.shape[:2]
    most = numbers.shape[0]
    members = mine * n
    part = slots // parts
    steps = most // GROUP
    obs_tiles = obs_all.shape[1] // TILE
    scale = 1.0 / (members - 1.0)
    margin = EDGE * TILE
    sources = (obs, res)
    targets = (obs_all, res_all)
    above = slab < slabs - 1
    below = slab > 0

    def rows(owner):
        return pl.ds(pl.multiple_of(owner * mine, 8), mine)

    def fore_rows(owner):
        return pl.ds(owner * groups, groups)

    middle = pl.ds(margin, points)
    low = pl.ds(0, margin)
    high = pl.ds(margin + points, margin)

    barrier = pltpu.get_barrier_semaphore()
    for k in range(1, n):
        pl.semaphore_signal(
            barrier, inc=1, device_id=(slab, flip(region, k)), device_id_type=MESH
        )

    for exists, other in ((above, slab + 1), (below, slab - 1)):

        @pl.when(exists)
        def _(other=other):
            for k in (0, 1):
                pl.semaphore_signal(
                    barrier, inc=1, device_id=(other, flip(region, k)), device_id_type=MESH
                )

    beside = above.astype(jnp.int32) + below.astype(jnp.int32)
    pl.semaphore_wait(barrier, n - 1 + 2 * beside)

    def edge_copies(k, side, other, act):
        block = rows(flip(region, k))
        for a in range(2):
            if k == 0:
                src = sources[a].at[:, pl.ds(points - margin, margin) if side == 0 else low]
            else:
                first = points if side == 0 else margin
                src = targets[a].at[block, pl.ds(first, margin)]
            for core in range(2):
                copy = pltpu.make_async_remote_copy(
                    src_ref=src,
                    dst_ref=targets[a].at[block, low if side == 0 else high],
                    send_sem=edge_send.at[side, a, k + core],
                    recv_sem=edge_recv.at[side, a, k + core],
                    device_id=(other, flip(region, core)),
                    device_id_type=MESH,
                )
                act(copy)

    def send_edges(k):
        for side, exists, other in ((0, above, slab + 1), (1, below, slab - 1)):

            @pl.when(exists)
            def _(side=side, other=other):
                edge_copies(k, side, other, lambda copy: copy.start())

    sent = []
    bits = [1 << b for b in range(1, n.bit_length() - 1)]

    def forward(k):
        for a in range(2):
            place = targets[a].at[rows(flip(region, k)), middle]
            src = sources[a] if k == 0 else place
            for bit in bits:
                to = k | bit
                last = [b for b in bits if b & to][-1 if a == 0 else 0]
                if k & bit or last != bit:
                    continue
                sent.append(
                    push(
                        src,
                        place,
                        near_send.at[a, to],
                        near_recv.at[a, to],
                        slab,
                        flip(region, bit),
                    )
                )
            sent.append(
                push(src, place, near_send.at[a, k + 1], near_recv.at[a, k + 1], slab, flip(region, 1))
            )

    def near_wait(a, k):
        place = targets[a].at[rows(flip(region, k)), middle]
        pltpu.make_async_copy(place, place, near_recv.at[a, k]).wait()

    def send_fore():
        for g in range(parts):
            some = pl.ds(g * part, part)
            for k in [*range(2, n), 1]:
                sent.append(
                    push(
                        prior.at[:, some, flip(region, k)],
                        fore.at[fore_rows(region), some],
                        fore_send.at[g, k],
                        fore_recv.at[g, k],
                        slab,
                        flip(region, k),
                    )
                )

    last_tile = oxy.shape[1] // TILE - 1
    first_tile = slab * (points // TILE) - EDGE

    def spread(q, carry):
        place = jnp.clip(first_tile + q, 0, last_tile)
        there = pl.ds(pl.multiple_of(place * TILE, TILE), TILE)
        ox[q] = jnp.broadcast_to(oxy[0:1, there], (TILE, TILE)).T
        oy[q] = jnp.broadcast_to(oxy[1:2, there], (TILE, TILE)).T
        return carry

    def taper_slot(slot, carry):
        tile = slot * n + region
        columns = pl.ds(pl.multiple_of(tile * TILE, TILE), TILE)
        gx = gxy[0:1, columns]
        gy = gxy[1:2, columns]
        count = totals[tile]

        def one(p, inner):
            q = numbers[p, tile]
            away = jnp.where(p < count, 0.0, 64.0)
            tapers[slot * most + p] = taper_of(gx + away, gy, ox[q], oy[q])
            return inner

        return lax.fori_loop(0, most, one, carry)

    forward(0)
    send_edges(0)
    own = [
        pltpu.make_async_copy(sources[a], targets[a].at[rows(region), middle], own_sem.at[a])
        for a in range(2)
    ]
    own.append(pltpu.make_async_copy(prior.at[:, :, region], fore.at[fore_rows(region)], own_sem.at[2]))
    for copy in own:
        copy.start()

    for exists, columns in ((below, low), (above, high)):

        @pl.when(jnp.logical_not(exists))
        def _(columns=columns):
            for a in range(2):
                targets[a][:, columns] = jnp.zeros((members, margin), jnp.float32)

    half, most_of = slots // 2, 3 * slots // 4
    lax.fori_loop(0, obs_tiles, spread, 0)
    lax.fori_loop(0, half, taper_slot, 0)
    even = sorted(range(2, n, 2), key=lambda k: (k.bit_count(), k))
    single = [k for k in even if k.bit_count() == 1]
    for k in even:
        for a in range(2):
            near_wait(a, k)
        forward(k)
        send_edges(k)
        if k == single[-1]:
            lax.fori_loop(half, most_of, taper_slot, 0)
    send_fore()
    lax.fori_loop(most_of, slots, taper_slot, 0)

    for k in range(1, n, 2):
        for a in range(2):
            near_wait(a, k)
    for side, comes in ((0, below), (1, above)):

        @pl.when(comes)
        def _(side=side):
            for k in range(n):
                for a in range(2):
                    place = targets[a].at[rows(flip(region, k)), low if side == 0 else high]
                    pltpu.make_async_copy(place, place, edge_recv.at[side, a, k]).wait()

    for copy in own[:2]:
        copy.wait()

    def prepare(q, carry):
        columns = pl.ds(pl.multiple_of(q * TILE, TILE), TILE)
        values = obs_all[:, columns]
        values = values - jnp.mean(values, axis=0, keepdims=True)
        high, low = split(values.T)
        ot[q, :TILE, :] = high
        ot[q, TILE:, :] = low
        high, low = split(res_all[:, columns])
        rr[q, :, :TILE] = high
        rr[q, :, TILE:] = low
        return carry

    lax.fori_loop(0, obs_tiles, prepare, 0)
    own[2].wait()

    def prepare_fore(slot, carry):
        values = fore[:, slot].reshape(members, TILE)
        values = (values - jnp.mean(values, axis=0, keepdims=True)) * scale
        high, low = split(values)
        ff[slot, :, :TILE] = high
        ff[slot, :, TILE:] = low
        increment[:, slot] = jnp.zeros((members // 8, 8, TILE), jnp.float32)
        return carry

    def spend(slot, step):
        tile = slot * n + region
        found = [numbers[step * GROUP + k, tile] for k in range(GROUP)]
        weights = held[...]
        both = dot(jnp.concatenate([rr[q, :, :TILE] for q in found], axis=1), weights)
        rest = dot(jnp.concatenate([rr[q, :, TILE:] for q in found], axis=1), weights[:, :TILE])
        return both[:, :TILE] + (both[:, TILE:] + rest)

    def store(slot, term):
        increment[:, slot] += term.reshape(members // 8, 8, TILE)

    for g in range(parts):
        some = pl.ds(g * part, part)
        for k in range(1, n):
            place = fore.at[fore_rows(flip(region, k)), some]
            pltpu.make_async_copy(place, place, fore_recv.at[g, k]).wait()
        lax.fori_loop(g * part, (g + 1) * part, prepare_fore, 0)
        held[...] = jnp.zeros_like(held)

        def body(turn, carry, start=g * part):
            slot = start + turn // steps
            step = turn % steps
            before = jnp.maximum(turn - 1, 0)
            old = start + before // steps
            term = spend(old, before % steps)
            tile = slot * n + region
            made = []
            for k in range(GROUP):
                p = step * GROUP + k
                q = numbers[p, tile]
                four = dot(ot[q], ff[slot])
                covariance = four[:TILE, :TILE] + (four[:TILE, TILE:] + four[TILE:, :TILE])
                made.append(split(tapers[slot * most + p] * covariance))
            for k in range(GROUP):
                held[k * TILE : (k + 1) * TILE, :TILE] = made[k][0]
                held[k * TILE : (k + 1) * TILE, TILE:] = made[k][1]
            store(old, term)
            return carry

        lax.fori_loop(0, part * steps, body, 0)
        store((g + 1) * part - 1, spend((g + 1) * part - 1, steps - 1))
        for k in [*range(2, n), 1]:
            other = flip(region, k)
            sent.append(
                push(
                    increment.at[fore_rows(other), some],
                    back.at[:, some, region],
                    back_send.at[g, k],
                    back_recv.at[g, k],
                    slab,
                    other,
                )
            )
        own.append(
            pltpu.make_async_copy(
                increment.at[fore_rows(region), some], back.at[:, some, region], own_sem.at[3 + g]
            )
        )
        own[-1].start()

    for g in range(parts):
        for k in range(1, n):
            place = back.at[:, pl.ds(g * part, part), flip(region, k)]
            pltpu.make_async_copy(place, place, back_recv.at[g, k]).wait()

    for side, exists, other in ((0, above, slab + 1), (1, below, slab - 1)):

        @pl.when(exists)
        def _(side=side, other=other):
            for k in range(0, n, 2):
                edge_copies(k, side, other, lambda copy: copy.wait_send())

    for copy in sent:
        copy.wait_send()
    for copy in own[3:]:
        copy.wait()


def analyse(n, slabs, totals, numbers, prior, obs, res, gxy, oxy):
    groups, slots = prior.shape[:2]
    mine, points = obs.shape
    most = numbers.shape[0]
    members = mine * n
    parts = PARTS if slots % PARTS == 0 else 1
    obs_tiles = points // TILE + 2 * EDGE
    wide = pltpu.VMEM((members, points + 2 * EDGE * TILE), jnp.float32)
    tiles = pltpu.VMEM((groups * n, slots, 8, TILE), jnp.float32)
    spread = pltpu.VMEM((obs_tiles, TILE, TILE), jnp.float32)
    smem = pl.BlockSpec(memory_space=pltpu.SMEM)
    vmem = pl.BlockSpec(memory_space=pltpu.VMEM)
    hbm = pl.BlockSpec(memory_space=pltpu.HBM)
    dma = pltpu.SemaphoreType.DMA
    return pl.pallas_call(
        functools.partial(ensemble_kernel, n, slabs, parts),
        out_shape=jax.ShapeDtypeStruct((groups, slots, n, 8, TILE), jnp.float32),
        in_specs=[smem, smem, hbm, hbm, hbm, vmem, vmem],
        out_specs=pl.BlockSpec(memory_space=pl.ANY),
        scratch_shapes=[
            tiles,
            tiles,
            wide,
            wide,
            pltpu.VMEM((obs_tiles, 2 * TILE, members), jnp.bfloat16),
            pltpu.VMEM((obs_tiles, members, 2 * TILE), jnp.bfloat16),
            spread,
            spread,
            pltpu.VMEM((slots * most, TILE, TILE), jnp.float32),
            pltpu.VMEM((slots, members, 2 * TILE), jnp.bfloat16),
            pltpu.VMEM((GROUP * TILE, 2 * TILE), jnp.bfloat16),
            dma((3 + parts,)),
            dma((parts, n)),
            dma((parts, n)),
            dma((2, n)),
            dma((2, n)),
            dma((2, 2, n)),
            dma((2, 2, n)),
            dma((parts, n)),
            dma((parts, n)),
        ],
        compiler_params=pltpu.CompilerParams(
            collective_id=0, has_side_effects=True, vmem_limit_bytes=50 * 1024 * 1024
        ),
    )(totals, numbers, prior, obs, res, gxy, oxy)


def split(x):
    high = x.astype(jnp.bfloat16)
    low = (x - high.astype(jnp.float32)).astype(jnp.bfloat16)
    return high, low


def taper_of(gx, gy, ox, oy):
    dx = ox - gx
    dy = oy - gy
    d2 = dx * dx + dy * dy
    inv = lax.rsqrt(jnp.maximum(d2, 1e-30))
    z = d2 * inv
    a = 0.5 * d2 - 5.0 / 3.0
    near = d2 * (z * (0.625 - 0.25 * d2) + a) + 1.0
    far = d2 * (z * (0.625 + d2 * (1.0 / 12.0)) - a) + (4.0 - 5.0 * z) - (2.0 / 3.0) * inv
    return jnp.where(d2 <= 1.0, near, jnp.where(d2 <= 4.0, far, 0.0))


def dot(a, b):
    return lax.dot_general(a, b, (((1,), (0,)), ((), ())), preferred_element_type=jnp.float32)


def per_device(
    prior_matrix,
    prior_at_measurements,
    scaled_residual_vector,
    lattice_coordinates,
    measurement_coordinates,
    neighbour_block_totals,
    neighbour_block_numbers,
):
    regions = lax.axis_size("region")
    mine, points = prior_matrix.shape
    slots = neighbour_block_totals.shape[0] // regions
    blocks = prior_matrix.reshape(mine // 8, 8, slots, regions, TILE).transpose(0, 2, 3, 1, 4)
    back = analyse(
        regions,
        lax.axis_size("slab"),
        neighbour_block_totals,
        neighbour_block_numbers.T,
        blocks,
        prior_at_measurements,
        scaled_residual_vector,
        lattice_coordinates,
        measurement_coordinates,
    )
    return prior_matrix + back.transpose(0, 3, 1, 2, 4).reshape(mine, points)


def solution(mesh):
    in_specs = (
        P("region", "slab"),
        P("region", "slab"),
        P("region", "slab"),
        P(None, "slab"),
        P(),
        P("slab"),
        P("slab", None),
    )
    return jax.shard_map(
        per_device, mesh=mesh, in_specs=in_specs, out_specs=P("region", "slab"), check_vma=False
    )
```

```python
import functools

import jax
import jax.numpy as jnp
from jax import lax
from jax.experimental import pallas as pl
from jax.experimental.pallas import tpu as pltpu
from jax.sharding import PartitionSpec as P

TILE = 128
EDGE = 2
GROUP = 4
PARTS = 4
MESH = pl.DeviceIdType.MESH


def flip(index, bits):
    step = 1
    while step <= bits:
        if bits & step:
            index = index + step - 2 * step * ((index // step) % 2)
        step *= 2
    return index


def push(src, dst, send, recv, slab, region):
    copy = pltpu.make_async_remote_copy(
        src_ref=src,
        dst_ref=dst,
        send_sem=send,
        recv_sem=recv,
        device_id=(slab, region),
        device_id_type=MESH,
    )
    copy.start()
    return copy


def ensemble_kernel(
    n,
    slabs,
    parts,
    totals,
    numbers,
    prior,
    obs,
    res,
    gxy_all,
    oxy_all,
    back,
    gxy,
    oxy,
    fore,
    increment,
    obs_all,
    res_all,
    ot,
    rr,
    ox,
    oy,
    tapers,
    ff,
    held,
    own_sem,
    fore_send,
    fore_recv,
    near_send,
    near_recv,
    edge_send,
    edge_recv,
    back_send,
    back_recv,
):
    slab = lax.axis_index("slab")
    region = lax.axis_index("region")
    mine, points = obs.shape
    groups, slots = prior.shape[:2]
    most = numbers.shape[0]
    members = mine * n
    part = slots // parts
    steps = most // GROUP
    obs_tiles = obs_all.shape[1] // TILE
    scale = 1.0 / (members - 1.0)
    margin = EDGE * TILE
    sources = (obs, res)
    targets = (obs_all, res_all)
    above = slab < slabs - 1
    below = slab > 0

    def rows(owner):
        return pl.ds(pl.multiple_of(owner * mine, 8), mine)

    def fore_rows(owner):
        return pl.ds(owner * groups, groups)

    middle = pl.ds(margin, points)
    low = pl.ds(0, margin)
    high = pl.ds(margin + points, margin)

    places = [
        pltpu.make_async_copy(gxy_all, gxy, own_sem.at[3 + parts]),
        pltpu.make_async_copy(oxy_all, oxy, own_sem.at[4 + parts]),
    ]
    for copy in places:
        copy.start()

    barrier = pltpu.get_barrier_semaphore()
    for k in range(1, n):
        pl.semaphore_signal(
            barrier, inc=1, device_id=(slab, flip(region, k)), device_id_type=MESH
        )

    for exists, other in ((above, slab + 1), (below, slab - 1)):

        @pl.when(exists)
        def _(other=other):
            for k in (0, 1):
                pl.semaphore_signal(
                    barrier, inc=1, device_id=(other, flip(region, k)), device_id_type=MESH
                )

    beside = above.astype(jnp.int32) + below.astype(jnp.int32)
    pl.semaphore_wait(barrier, n - 1 + 2 * beside)

    def edge_copies(k, side, other, act):
        block = rows(flip(region, k))
        for a in range(2):
            if k == 0:
                src = sources[a].at[:, pl.ds(points - margin, margin) if side == 0 else low]
            else:
                first = points if side == 0 else margin
                src = targets[a].at[block, pl.ds(first, margin)]
            for core in range(2):
                copy = pltpu.make_async_remote_copy(
                    src_ref=src,
                    dst_ref=targets[a].at[block, low if side == 0 else high],
                    send_sem=edge_send.at[side, a, k + core],
                    recv_sem=edge_recv.at[side, a, k + core],
                    device_id=(other, flip(region, core)),
                    device_id_type=MESH,
                )
                act(copy)

    def send_edges(k):
        for side, exists, other in ((0, above, slab + 1), (1, below, slab - 1)):

            @pl.when(exists)
            def _(side=side, other=other):
                edge_copies(k, side, other, lambda copy: copy.start())

    sent = []
    bits = [1 << b for b in range(1, n.bit_length() - 1)]

    def forward(k):
        for a in range(2):
            place = targets[a].at[rows(flip(region, k)), middle]
            src = sources[a] if k == 0 else place
            for bit in bits:
                to = k | bit
                last = [b for b in bits if b & to][-1 if a == 0 else 0]
                if k & bit or last != bit:
                    continue
                sent.append(
                    push(
                        src,
                        place,
                        near_send.at[a, to],
                        near_recv.at[a, to],
                        slab,
                        flip(region, bit),
                    )
                )
            sent.append(
                push(src, place, near_send.at[a, k + 1], near_recv.at[a, k + 1], slab, flip(region, 1))
            )

    def near_wait(a, k):
        place = targets[a].at[rows(flip(region, k)), middle]
        pltpu.make_async_copy(place, place, near_recv.at[a, k]).wait()

    def send_fore():
        for g in range(parts):
            some = pl.ds(g * part, part)
            for k in [*range(2, n), 1]:
                sent.append(
                    push(
                        prior.at[:, some, flip(region, k)],
                        fore.at[fore_rows(region), some],
                        fore_send.at[g, k],
                        fore_recv.at[g, k],
                        slab,
                        flip(region, k),
                    )
                )

    last_tile = oxy.shape[1] // TILE - 1
    first_tile = slab * (points // TILE) - EDGE

    def spread(q, carry):
        place = jnp.clip(first_tile + q, 0, last_tile)
        there = pl.ds(pl.multiple_of(place * TILE, TILE), TILE)
        ox[q] = jnp.broadcast_to(oxy[0:1, there], (TILE, TILE)).T
        oy[q] = jnp.broadcast_to(oxy[1:2, there], (TILE, TILE)).T
        return carry

    def taper_slot(slot, carry):
        tile = slot * n + region
        columns = pl.ds(pl.multiple_of(tile * TILE, TILE), TILE)
        gx = gxy[0:1, columns]
        gy = gxy[1:2, columns]
        count = totals[tile]

        def one(p, inner):
            q = numbers[p, tile]
            away = jnp.where(p < count, 0.0, 64.0)
            tapers[slot * most + p] = taper_of(gx + away, gy, ox[q], oy[q])
            return inner

        return lax.fori_loop(0, most, one, carry)

    forward(0)
    send_edges(0)
    own = [
        pltpu.make_async_copy(sources[a], targets[a].at[rows(region), middle], own_sem.at[a])
        for a in range(2)
    ]
    own.append(pltpu.make_async_copy(prior.at[:, :, region], fore.at[fore_rows(region)], own_sem.at[2]))
    for copy in own:
        copy.start()

    for exists, columns in ((below, low), (above, high)):

        @pl.when(jnp.logical_not(exists))
        def _(columns=columns):
            for a in range(2):
                targets[a][:, columns] = jnp.zeros((members, margin), jnp.float32)

    half, most_of = slots // 2, 3 * slots // 4
    for copy in places:
        copy.wait()
    lax.fori_loop(0, obs_tiles, spread, 0)
    lax.fori_loop(0, half, taper_slot, 0)
    even = sorted(range(2, n, 2), key=lambda k: (k.bit_count(), k))
    single = [k for k in even if k.bit_count() == 1]
    for k in even:
        for a in range(2):
            near_wait(a, k)
        forward(k)
        send_edges(k)
        if k == single[-1]:
            lax.fori_loop(half, most_of, taper_slot, 0)
    send_fore()
    lax.fori_loop(most_of, slots, taper_slot, 0)

    for k in range(1, n, 2):
        for a in range(2):
            near_wait(a, k)
    for side, comes in ((0, below), (1, above)):

        @pl.when(comes)
        def _(side=side):
            for k in range(n):
                for a in range(2):
                    place = targets[a].at[rows(flip(region, k)), low if side == 0 else high]
                    pltpu.make_async_copy(place, place, edge_recv.at[side, a, k]).wait()

    for copy in own[:2]:
        copy.wait()

    def prepare(q, carry):
        columns = pl.ds(pl.multiple_of(q * TILE, TILE), TILE)
        values = obs_all[:, columns]
        values = values - jnp.mean(values, axis=0, keepdims=True)
        high, low = split(values.T)
        ot[q, :TILE, :] = high
        ot[q, TILE:, :] = low
        high, low = split(res_all[:, columns])
        rr[q, :, :TILE] = high
        rr[q, :, TILE:] = low
        return carry

    lax.fori_loop(0, obs_tiles, prepare, 0)
    own[2].wait()

    def prepare_fore(slot, carry):
        values = fore[:, slot].reshape(members, TILE)
        values = (values - jnp.mean(values, axis=0, keepdims=True)) * scale
        high, low = split(values)
        ff[slot, :, :TILE] = high
        ff[slot, :, TILE:] = low
        increment[:, slot] = jnp.zeros((members // 8, 8, TILE), jnp.float32)
        return carry

    def spend(slot, step):
        tile = slot * n + region
        found = [numbers[step * GROUP + k, tile] for k in range(GROUP)]
        weights = held[...]
        both = dot(
            jnp.concatenate(
                [
                    jnp.concatenate([rr[q, :, :TILE] for q in found], axis=1),
                    jnp.concatenate([rr[q, :, TILE:] for q in found], axis=1),
                ],
                axis=0,
            ),
            weights,
        )
        return both[:members, :TILE] + (both[:members, TILE:] + both[members:, :TILE])

    def store(slot, term):
        increment[:, slot] += term.reshape(members // 8, 8, TILE)

    for g in range(parts):
        some = pl.ds(g * part, part)
        for k in range(1, n):
            place = fore.at[fore_rows(flip(region, k)), some]
            pltpu.make_async_copy(place, place, fore_recv.at[g, k]).wait()
        lax.fori_loop(g * part, (g + 1) * part, prepare_fore, 0)
        held[...] = jnp.zeros_like(held)

        def body(turn, carry, start=g * part):
            slot = start + turn // steps
            step = turn % steps
            before = jnp.maximum(turn - 1, 0)
            old = start + before // steps
            term = spend(old, before % steps)
            tile = slot * n + region
            made = []
            listed = [ot[numbers[step * GROUP + k, tile]] for k in range(GROUP)]
            every = dot(jnp.concatenate(listed, axis=0), ff[slot])
            for k in range(GROUP):
                p = step * GROUP + k
                four = every[2 * TILE * k : 2 * TILE * (k + 1)]
                covariance = four[:TILE, :TILE] + (four[:TILE, TILE:] + four[TILE:, :TILE])
                made.append(split(tapers[slot * most + p] * covariance))
            for k in range(GROUP):
                held[k * TILE : (k + 1) * TILE, :TILE] = made[k][0]
                held[k * TILE : (k + 1) * TILE, TILE:] = made[k][1]
            store(old, term)
            return carry

        lax.fori_loop(0, part * steps, body, 0)
        store((g + 1) * part - 1, spend((g + 1) * part - 1, steps - 1))
        for k in [*range(2, n), 1]:
            other = flip(region, k)
            sent.append(
                push(
                    increment.at[fore_rows(other), some],
                    back.at[:, some, region],
                    back_send.at[g, k],
                    back_recv.at[g, k],
                    slab,
                    other,
                )
            )
        own.append(
            pltpu.make_async_copy(
                increment.at[fore_rows(region), some], back.at[:, some, region], own_sem.at[3 + g]
            )
        )
        own[-1].start()

    for g in range(parts):
        for k in range(1, n):
            place = back.at[:, pl.ds(g * part, part), flip(region, k)]
            pltpu.make_async_copy(place, place, back_recv.at[g, k]).wait()

    for side, exists, other in ((0, above, slab + 1), (1, below, slab - 1)):

        @pl.when(exists)
        def _(side=side, other=other):
            for k in range(0, n, 2):
                edge_copies(k, side, other, lambda copy: copy.wait_send())

    for copy in sent:
        copy.wait_send()
    for copy in own[3:]:
        copy.wait()


def analyse(n, slabs, totals, numbers, prior, obs, res, gxy, oxy):
    groups, slots = prior.shape[:2]
    mine, points = obs.shape
    most = numbers.shape[0]
    members = mine * n
    parts = PARTS if slots % PARTS == 0 else 1
    obs_tiles = points // TILE + 2 * EDGE
    wide = pltpu.VMEM((members, points + 2 * EDGE * TILE), jnp.float32)
    tiles = pltpu.VMEM((groups * n, slots, 8, TILE), jnp.float32)
    spread = pltpu.VMEM((obs_tiles, TILE, TILE), jnp.float32)
    smem = pl.BlockSpec(memory_space=pltpu.SMEM)
    hbm = pl.BlockSpec(memory_space=pltpu.HBM)
    dma = pltpu.SemaphoreType.DMA
    return pl.pallas_call(
        functools.partial(ensemble_kernel, n, slabs, parts),
        out_shape=jax.ShapeDtypeStruct((groups, slots, n, 8, TILE), jnp.float32),
        in_specs=[smem, smem, hbm, hbm, hbm, hbm, hbm],
        out_specs=pl.BlockSpec(memory_space=pl.ANY),
        scratch_shapes=[
            pltpu.VMEM(gxy.shape, jnp.float32),
            pltpu.VMEM(oxy.shape, jnp.float32),
            tiles,
            tiles,
            wide,
            wide,
            pltpu.VMEM((obs_tiles, 2 * TILE, members), jnp.bfloat16),
            pltpu.VMEM((obs_tiles, members, 2 * TILE), jnp.bfloat16),
            spread,
            spread,
            pltpu.VMEM((slots * most, TILE, TILE), jnp.float32),
            pltpu.VMEM((slots, members, 2 * TILE), jnp.bfloat16),
            pltpu.VMEM((GROUP * TILE, 2 * TILE), jnp.bfloat16),
            dma((5 + parts,)),
            dma((parts, n)),
            dma((parts, n)),
            dma((2, n)),
            dma((2, n)),
            dma((2, 2, n)),
            dma((2, 2, n)),
            dma((parts, n)),
            dma((parts, n)),
        ],
        compiler_params=pltpu.CompilerParams(
            collective_id=0, has_side_effects=True, vmem_limit_bytes=62 * 1024 * 1024
        ),
    )(totals, numbers, prior, obs, res, gxy, oxy)


def split(x):
    high = x.astype(jnp.bfloat16)
    low = (x - high.astype(jnp.float32)).astype(jnp.bfloat16)
    return high, low


def taper_of(gx, gy, ox, oy):
    dx = ox - gx
    dy = oy - gy
    d2 = dx * dx + dy * dy
    inv = lax.rsqrt(jnp.maximum(d2, 1e-30))
    z = d2 * inv
    near = d2 * (z * (0.625 - 0.25 * d2) + (0.5 * d2 - 5.0 / 3.0)) + 1.0
    rest = jnp.maximum(2.0 - z, 0.0)
    square = rest * rest
    far = (square * square) * (z * (z * (1.0 / 12.0) + 1.0 / 6.0) - 1.0 / 24.0) * inv
    return jnp.where(d2 <= 1.0, near, far)


def dot(a, b):
    return lax.dot_general(a, b, (((1,), (0,)), ((), ())), preferred_element_type=jnp.float32)


def per_device(
    prior_matrix,
    prior_at_measurements,
    scaled_residual_vector,
    lattice_coordinates,
    measurement_coordinates,
    neighbour_block_totals,
    neighbour_block_numbers,
):
    regions = lax.axis_size("region")
    mine, points = prior_matrix.shape
    slots = neighbour_block_totals.shape[0] // regions
    blocks = prior_matrix.reshape(mine // 8, 8, slots, regions, TILE).transpose(0, 2, 3, 1, 4)
    back = analyse(
        regions,
        lax.axis_size("slab"),
        neighbour_block_totals,
        neighbour_block_numbers.T,
        blocks,
        prior_at_measurements,
        scaled_residual_vector,
        lattice_coordinates,
        measurement_coordinates,
    )
    return prior_matrix + back.transpose(0, 3, 1, 2, 4).reshape(mine, points)


def solution(mesh):
    in_specs = (
        P("region", "slab"),
        P("region", "slab"),
        P("region", "slab"),
        P(None, "slab"),
        P(),
        P("slab"),
        P("slab", None),
    )
    return jax.shard_map(
        per_device, mesh=mesh, in_specs=in_specs, out_specs=P("region", "slab"), check_vma=False
    )
```

```python
import functools

import jax
import jax.numpy as jnp
from jax import lax
from jax.experimental import pallas as pl
from jax.experimental.pallas import tpu as pltpu
from jax.sharding import PartitionSpec as P

TILE = 128
EDGE = 2
GROUP = 4
PARTS = 4
MESH = pl.DeviceIdType.MESH


def flip(index, bits):
    step = 1
    while step <= bits:
        if bits & step:
            index = index + step - 2 * step * ((index // step) % 2)
        step *= 2
    return index


def push(src, dst, send, recv, slab, region):
    copy = pltpu.make_async_remote_copy(
        src_ref=src,
        dst_ref=dst,
        send_sem=send,
        recv_sem=recv,
        device_id=(slab, region),
        device_id_type=MESH,
    )
    copy.start()
    return copy


def ensemble_kernel(
    n,
    slabs,
    parts,
    totals,
    numbers,
    prior,
    obs,
    res,
    gxy_all,
    oxy_all,
    back,
    gxy,
    oxy,
    fore,
    increment,
    obs_all,
    res_all,
    ot,
    rr,
    ox,
    oy,
    tapers,
    ff,
    held,
    own_sem,
    fore_send,
    fore_recv,
    near_send,
    near_recv,
    edge_send,
    edge_recv,
    back_send,
    back_recv,
):
    slab = lax.axis_index("slab")
    region = lax.axis_index("region")
    mine, points = obs.shape
    groups, slots = prior.shape[:2]
    most = numbers.shape[0]
    members = mine * n
    part = slots // parts
    steps = most // GROUP
    obs_tiles = obs_all.shape[1] // TILE
    scale = 1.0 / (members - 1.0)
    margin = EDGE * TILE
    sources = (obs, res)
    targets = (obs_all, res_all)
    above = slab < slabs - 1
    below = slab > 0

    def rows(owner):
        return pl.ds(pl.multiple_of(owner * mine, 8), mine)

    def fore_rows(owner):
        return pl.ds(owner * groups, groups)

    middle = pl.ds(margin, points)
    low = pl.ds(0, margin)
    high = pl.ds(margin + points, margin)

    places = [
        pltpu.make_async_copy(gxy_all, gxy, own_sem.at[3 + parts]),
        pltpu.make_async_copy(oxy_all, oxy, own_sem.at[4 + parts]),
    ]
    for copy in places:
        copy.start()

    barrier = pltpu.get_barrier_semaphore()
    for k in range(1, n):
        pl.semaphore_signal(
            barrier, inc=1, device_id=(slab, flip(region, k)), device_id_type=MESH
        )

    for exists, other in ((above, slab + 1), (below, slab - 1)):

        @pl.when(exists)
        def _(other=other):
            for k in (0, 1):
                pl.semaphore_signal(
                    barrier, inc=1, device_id=(other, flip(region, k)), device_id_type=MESH
                )

    beside = above.astype(jnp.int32) + below.astype(jnp.int32)
    pl.semaphore_wait(barrier, n - 1 + 2 * beside)

    def edge_copies(k, side, other, act):
        block = rows(flip(region, k))
        for a in range(2):
            if k == 0:
                src = sources[a].at[:, pl.ds(points - margin, margin) if side == 0 else low]
            else:
                first = points if side == 0 else margin
                src = targets[a].at[block, pl.ds(first, margin)]
            for core in range(2):
                copy = pltpu.make_async_remote_copy(
                    src_ref=src,
                    dst_ref=targets[a].at[block, low if side == 0 else high],
                    send_sem=edge_send.at[side, a, k + core],
                    recv_sem=edge_recv.at[side, a, k + core],
                    device_id=(other, flip(region, core)),
                    device_id_type=MESH,
                )
                act(copy)

    def send_edges(k):
        for side, exists, other in ((0, above, slab + 1), (1, below, slab - 1)):

            @pl.when(exists)
            def _(side=side, other=other):
                edge_copies(k, side, other, lambda copy: copy.start())

    sent = []
    bits = [1 << b for b in range(1, n.bit_length() - 1)]

    def forward(k):
        for a in range(2):
            place = targets[a].at[rows(flip(region, k)), middle]
            src = sources[a] if k == 0 else place
            for bit in bits:
                to = k | bit
                last = [b for b in bits if b & to][-1 if a == 0 else 0]
                if k & bit or last != bit:
                    continue
                sent.append(
                    push(
                        src,
                        place,
                        near_send.at[a, to],
                        near_recv.at[a, to],
                        slab,
                        flip(region, bit),
                    )
                )
            sent.append(
                push(src, place, near_send.at[a, k + 1], near_recv.at[a, k + 1], slab, flip(region, 1))
            )

    def near_wait(a, k):
        place = targets[a].at[rows(flip(region, k)), middle]
        pltpu.make_async_copy(place, place, near_recv.at[a, k]).wait()

    def send_fore():
        for g in range(parts):
            some = pl.ds(g * part, part)
            for k in [*range(2, n), 1]:
                sent.append(
                    push(
                        prior.at[:, some, flip(region, k)],
                        fore.at[fore_rows(region), some],
                        fore_send.at[g, k],
                        fore_recv.at[g, k],
                        slab,
                        flip(region, k),
                    )
                )

    last_tile = oxy.shape[1] // TILE - 1
    first_tile = slab * (points // TILE) - EDGE

    def spread(q, carry):
        place = jnp.clip(first_tile + q, 0, last_tile)
        there = pl.ds(pl.multiple_of(place * TILE, TILE), TILE)
        ox[q] = jnp.broadcast_to(oxy[0:1, there], (TILE, TILE)).T
        oy[q] = jnp.broadcast_to(oxy[1:2, there], (TILE, TILE)).T
        return carry

    def taper_slot(slot, carry):
        tile = slot * n + region
        columns = pl.ds(pl.multiple_of(tile * TILE, TILE), TILE)
        gx = gxy[0:1, columns]
        gy = gxy[1:2, columns]
        count = totals[tile]

        def one(p, inner):
            q = numbers[p, tile]
            away = jnp.where(p < count, 0.0, 64.0)
            tapers[slot * most + p] = taper_of(gx + away, gy, ox[q], oy[q])
            return inner

        return lax.fori_loop(0, most, one, carry)

    forward(0)
    send_edges(0)
    own = [
        pltpu.make_async_copy(sources[a], targets[a].at[rows(region), middle], own_sem.at[a])
        for a in range(2)
    ]
    own.append(pltpu.make_async_copy(prior.at[:, :, region], fore.at[fore_rows(region)], own_sem.at[2]))
    for copy in own:
        copy.start()

    for exists, columns in ((below, low), (above, high)):

        @pl.when(jnp.logical_not(exists))
        def _(columns=columns):
            for a in range(2):
                targets[a][:, columns] = jnp.zeros((members, margin), jnp.float32)

    half, most_of = slots // 2, 3 * slots // 4
    for copy in places:
        copy.wait()
    lax.fori_loop(0, obs_tiles, spread, 0)
    lax.fori_loop(0, half, taper_slot, 0)
    even = sorted(range(2, n, 2), key=lambda k: (k.bit_count(), k))
    single = [k for k in even if k.bit_count() == 1]
    for k in even:
        for a in range(2):
            near_wait(a, k)
        forward(k)
        send_edges(k)
        if k == single[-1]:
            lax.fori_loop(half, most_of, taper_slot, 0)
    send_fore()
    lax.fori_loop(most_of, slots, taper_slot, 0)

    for k in range(1, n, 2):
        for a in range(2):
            near_wait(a, k)
    for side, comes in ((0, below), (1, above)):

        @pl.when(comes)
        def _(side=side):
            for k in range(n):
                for a in range(2):
                    place = targets[a].at[rows(flip(region, k)), low if side == 0 else high]
                    pltpu.make_async_copy(place, place, edge_recv.at[side, a, k]).wait()

    for copy in own[:2]:
        copy.wait()

    def prepare(q, carry):
        columns = pl.ds(pl.multiple_of(q * TILE, TILE), TILE)
        values = obs_all[:, columns]
        values = values - jnp.mean(values, axis=0, keepdims=True)
        high, low = split(values.T)
        ot[q, :TILE, :] = high
        ot[q, TILE:, :] = low
        high, low = split(res_all[:, columns])
        rr[q, :, :TILE] = high
        rr[q, :, TILE:] = low
        return carry

    lax.fori_loop(0, obs_tiles, prepare, 0)
    own[2].wait()

    def prepare_fore(slot, carry):
        values = fore[:, slot].reshape(members, TILE)
        values = (values - jnp.mean(values, axis=0, keepdims=True)) * scale
        high, low = split(values)
        ff[slot, :, :TILE] = high
        ff[slot, :, TILE:] = low
        increment[:, slot] = jnp.zeros((members // 8, 8, TILE), jnp.float32)
        return carry

    def spend(slot, step):
        tile = slot * n + region
        found = [numbers[step * GROUP + k, tile] for k in range(GROUP)]
        weights = held[...]
        both = dot(jnp.concatenate([rr[q, :, :TILE] for q in found], axis=1), weights)
        rest = dot(jnp.concatenate([rr[q, :, TILE:] for q in found], axis=1), weights[:, :TILE])
        return both[:, :TILE] + (both[:, TILE:] + rest)

    def store(slot, term):
        increment[:, slot] += term.reshape(members // 8, 8, TILE)

    for g in range(parts):
        some = pl.ds(g * part, part)
        for k in range(1, n):
            place = fore.at[fore_rows(flip(region, k)), some]
            pltpu.make_async_copy(place, place, fore_recv.at[g, k]).wait()
        lax.fori_loop(g * part, (g + 1) * part, prepare_fore, 0)
        held[...] = jnp.zeros_like(held)

        def body(turn, carry, start=g * part):
            slot = start + turn // steps
            step = turn % steps
            before = jnp.maximum(turn - 1, 0)
            old = start + before // steps
            term = spend(old, before % steps)
            tile = slot * n + region
            made = []
            for k in range(GROUP):
                p = step * GROUP + k
                four = dot(ot[numbers[p, tile]], ff[slot])
                covariance = four[:TILE, :TILE] + (four[:TILE, TILE:] + four[TILE:, :TILE])
                made.append(split(tapers[slot * most + p] * covariance))
            for k in range(GROUP):
                held[k * TILE : (k + 1) * TILE, :TILE] = made[k][0]
                held[k * TILE : (k + 1) * TILE, TILE:] = made[k][1]
            store(old, term)
            return carry

        lax.fori_loop(0, part * steps, body, 0)
        store((g + 1) * part - 1, spend((g + 1) * part - 1, steps - 1))
        for k in [*range(2, n), 1]:
            other = flip(region, k)
            sent.append(
                push(
                    increment.at[fore_rows(other), some],
                    back.at[:, some, region],
                    back_send.at[g, k],
                    back_recv.at[g, k],
                    slab,
                    other,
                )
            )
        own.append(
            pltpu.make_async_copy(
                increment.at[fore_rows(region), some], back.at[:, some, region], own_sem.at[3 + g]
            )
        )
        own[-1].start()

    for g in range(parts):
        for k in range(1, n):
            place = back.at[:, pl.ds(g * part, part), flip(region, k)]
            pltpu.make_async_copy(place, place, back_recv.at[g, k]).wait()

    for side, exists, other in ((0, above, slab + 1), (1, below, slab - 1)):

        @pl.when(exists)
        def _(side=side, other=other):
            for k in range(0, n, 2):
                edge_copies(k, side, other, lambda copy: copy.wait_send())

    for copy in sent:
        copy.wait_send()
    for copy in own[3:]:
        copy.wait()


def analyse(n, slabs, totals, numbers, prior, obs, res, gxy, oxy):
    groups, slots = prior.shape[:2]
    mine, points = obs.shape
    most = numbers.shape[0]
    members = mine * n
    parts = PARTS if slots % PARTS == 0 else 1
    obs_tiles = points // TILE + 2 * EDGE
    wide = pltpu.VMEM((members, points + 2 * EDGE * TILE), jnp.float32)
    tiles = pltpu.VMEM((groups * n, slots, 8, TILE), jnp.float32)
    spread = pltpu.VMEM((obs_tiles, TILE, TILE), jnp.float32)
    smem = pl.BlockSpec(memory_space=pltpu.SMEM)
    hbm = pl.BlockSpec(memory_space=pltpu.HBM)
    dma = pltpu.SemaphoreType.DMA
    return pl.pallas_call(
        functools.partial(ensemble_kernel, n, slabs, parts),
        out_shape=jax.ShapeDtypeStruct((groups, slots, n, 8, TILE), jnp.float32),
        in_specs=[smem, smem, hbm, hbm, hbm, hbm, hbm],
        out_specs=pl.BlockSpec(memory_space=pl.ANY),
        scratch_shapes=[
            pltpu.VMEM(gxy.shape, jnp.float32),
            pltpu.VMEM(oxy.shape, jnp.float32),
            tiles,
            tiles,
            wide,
            wide,
            pltpu.VMEM((obs_tiles, 2 * TILE, members), jnp.bfloat16),
            pltpu.VMEM((obs_tiles, members, 2 * TILE), jnp.bfloat16),
            spread,
            spread,
            pltpu.VMEM((slots * most, TILE, TILE), jnp.float32),
            pltpu.VMEM((slots, members, 2 * TILE), jnp.bfloat16),
            pltpu.VMEM((GROUP * TILE, 2 * TILE), jnp.bfloat16),
            dma((5 + parts,)),
            dma((parts, n)),
            dma((parts, n)),
            dma((2, n)),
            dma((2, n)),
            dma((2, 2, n)),
            dma((2, 2, n)),
            dma((parts, n)),
            dma((parts, n)),
        ],
        compiler_params=pltpu.CompilerParams(
            collective_id=0, has_side_effects=True, vmem_limit_bytes=62 * 1024 * 1024
        ),
    )(totals, numbers, prior, obs, res, gxy, oxy)


def split(x):
    high = x.astype(jnp.bfloat16)
    low = (x - high.astype(jnp.float32)).astype(jnp.bfloat16)
    return high, low


def taper_of(gx, gy, ox, oy):
    dx = ox - gx
    dy = oy - gy
    d2 = dx * dx + dy * dy
    inv = lax.rsqrt(jnp.maximum(d2, 1e-30))
    z = d2 * inv
    near = d2 * (z * (0.625 - 0.25 * d2) + (0.5 * d2 - 5.0 / 3.0)) + 1.0
    rest = jnp.maximum(2.0 - z, 0.0)
    square = rest * rest
    far = (square * square) * (z * (z * (1.0 / 12.0) + 1.0 / 6.0) - 1.0 / 24.0) * inv
    return jnp.where(d2 <= 1.0, near, far)


def dot(a, b):
    return lax.dot_general(a, b, (((1,), (0,)), ((), ())), preferred_element_type=jnp.float32)


def per_device(
    prior_matrix,
    prior_at_measurements,
    scaled_residual_vector,
    lattice_coordinates,
    measurement_coordinates,
    neighbour_block_totals,
    neighbour_block_numbers,
):
    regions = lax.axis_size("region")
    mine, points = prior_matrix.shape
    slots = neighbour_block_totals.shape[0] // regions
    blocks = prior_matrix.reshape(mine // 8, 8, slots, regions, TILE).transpose(0, 2, 3, 1, 4)
    back = analyse(
        regions,
        lax.axis_size("slab"),
        neighbour_block_totals,
        neighbour_block_numbers.T,
        blocks,
        prior_at_measurements,
        scaled_residual_vector,
        lattice_coordinates,
        measurement_coordinates,
    )
    return prior_matrix + back.transpose(0, 3, 1, 2, 4).reshape(mine, points)


def solution(mesh):
    in_specs = (
        P("region", "slab"),
        P("region", "slab"),
        P("region", "slab"),
        P(None, "slab"),
        P(),
        P("slab"),
        P("slab", None),
    )
    return jax.shard_map(
        per_device, mesh=mesh, in_specs=in_specs, out_specs=P("region", "slab"), check_vma=False
    )
```
